32 devices in a mesh: grp: 2 (over y), freq: 4 (over z), shot: 2 (over x), rcv: 2 (over core).
Axes of the slice: x: 2, y: 2, z: 4, core: 2. Of those that a mesh axis runs over, the one named last changes fastest.
Arguments:
- data: bfloat16 [2, 256, 32, 4096], P(None, 'freq', ('grp', 'shot'), 'rcv'), parts along dimension 2, may hold values from -6 to 6
- estimate: bfloat16 [2, 256, 32, 4096], P(None, 'freq', ('grp', 'shot'), 'rcv'), parts along dimension 2, may hold values from -0.09375 to 0.09375
- window_data: bfloat16 [2, 256, 32, 16], P(None, 'freq', ('grp', 'shot')), parts along dimension 2, may hold values from -6 to 6
- wavelet: float32 [2, 512], P(None, ('grp', 'freq')), parts along dimension 1, may hold values from -24 to 24
- positions: int32 [32], P(('grp', 'shot')), parts along dimension 0, may hold values from 0 to 4095
- bins: int32 [512], P('grp'), parts along dimension 0, may hold values from 0 to 399
- threshold: int32 [2], P('grp'), parts along dimension 0, may hold values from 8 to 40
- step: float32 [2], P('grp'), parts along dimension 0, may hold values from 0.25 to 1
Outputs:
- primaries: bfloat16 [1024, 32, 4096], P('freq', ('grp', 'shot'), 'rcv'), parts along dimension 1
The draws below stay inside these ranges and needn't reach their ends.
There are 2 independent parts, one for each index of `grp`. The reference program is written for one: setup_inputs(seed, part) draws one part's arguments, and reference() takes and returns one part's arrays. A program takes and returns all parts, laid end to end along the dimension named above; each array names one. Nothing has to cross between parts.
All inputs are finite; a program needn't handle non-finite values.
Results may differ from the reference program's by a relative error of at most 0.0059.
The reference program's roundings to bfloat16 on the way count: a program that leaves them out, or rounds other values in their place, can miss the bound.
Values may be sent and summed in bfloat16 or wider, within the bound.
A program may use at most 64 MiB of HBM per device.

```python
import math
import jax
import jax.numpy as jnp
from jax import lax

NF = 256
RCV = 4096
NT = 1024
NBIN = 400
ROWS = 16
SHOTS = 16


def touch_ends(result, stream_key, smallest, top_value):
    extent = result.shape
    index_at = [jax.random.randint(jax.random.fold_in(stream_key, axis), (), 0, extent[axis]) for axis in range(len(extent))]
    result = result.at[tuple(index_at)].set(smallest)
    longest = extent.index(max(extent))
    index_at[longest] = (index_at[longest] + 1) % extent[longest]
    return result.at[tuple(index_at)].set(top_value)


def steps_of(own_key, extent, split, smallest, high):
    loudness, own = 1.0, jax.random.fold_in(own_key, 6)
    for axis_at, blocks in split:
        heights = jnp.exp(jax.random.uniform(jax.random.fold_in(own, axis_at), (blocks,), jnp.float32, smallest / len(split), high / len(split)))
        loudness = loudness * jnp.repeat(heights, extent[axis_at] // blocks).reshape([-1 if axis == axis_at else 1 for axis in range(len(extent))])
    return loudness


def scatter_about(own_key, extent, spread, reach, pieces=(), kind=jnp.bfloat16):
    gain = steps_of(own_key, extent, pieces, -0.22, 0.18) if pieces else 1.0
    array = jax.random.normal(own_key, extent, jnp.float32) * spread * gain
    return jnp.minimum(jnp.maximum(array, -reach), reach).astype(kind)


def setup_inputs(seed: int = 0, part: int = 0) -> dict:
    keys = jax.random.split(jax.random.key(seed), 9)
    part_splits = jax.random.split(jax.random.fold_in(keys[8], part), 9)
    return {
        "data": scatter_about(part_splits[0], (2, NF, SHOTS, RCV), 1.0, 6.0, ((1, 4), (2, 2), (3, 2))),
        "estimate": scatter_about(part_splits[1], (2, NF, ROWS, RCV), RCV ** -0.5, 0.09375, ((1, 4), (2, 2), (3, 2))),
        "window_data": scatter_about(part_splits[2], (2, NF, ROWS, SHOTS), 1.0, 6.0, ((1, 4), (2, 2))),
        "wavelet": scatter_about(part_splits[3], (2, NF), 4.0, 24.0, ((1, 4),), jnp.float32),
        "positions": touch_ends(jax.random.randint(part_splits[4], (SHOTS,), 0, RCV), jax.random.fold_in(part_splits[4], 1), 0, RCV - 1).astype(jnp.int32),
        "bins": touch_ends(jax.random.randint(part_splits[5], (NF,), 0, NBIN), jax.random.fold_in(part_splits[5], 1), 0, NBIN - 1).astype(jnp.int32),
        "threshold": jax.random.randint(part_splits[6], (1,), 8, 41).astype(jnp.int32),
        "step": jnp.clip(jnp.exp(jax.random.uniform(part_splits[7], (1,), jnp.float32, math.log(0.25), math.log(1.0))), 0.25, 1.0),
    }


def reference(data, estimate, window_data, wavelet, positions, bins, threshold, step):
    norm = 1.0 / math.sqrt(SHOTS * RCV)
    step_size = step[0]
    select = (jnp.arange(RCV, dtype=jnp.int32)[None, :] == positions[:, None]).astype(jnp.float32)

    def per_freq(items):
        est_re, est_im, line_re, line_im, rec_re, rec_im, source = items
        down_re = (source[0] * select - line_re.astype(jnp.float32)).astype(jnp.bfloat16)
        down_im = (source[1] * select - line_im.astype(jnp.float32)).astype(jnp.bfloat16)
        model_re = jnp.dot(est_re, down_re.T, preferred_element_type=jnp.float32) - jnp.dot(est_im, down_im.T, preferred_element_type=jnp.float32)
        model_im = jnp.dot(est_re, down_im.T, preferred_element_type=jnp.float32) + jnp.dot(est_im, down_re.T, preferred_element_type=jnp.float32)
        err_re = (rec_re.astype(jnp.float32) - model_re).astype(jnp.bfloat16)
        err_im = (rec_im.astype(jnp.float32) - model_im).astype(jnp.bfloat16)
        grad_re = jnp.dot(err_re, down_re, preferred_element_type=jnp.float32) + jnp.dot(err_im, down_im, preferred_element_type=jnp.float32)
        grad_im = jnp.dot(err_im, down_re, preferred_element_type=jnp.float32) - jnp.dot(err_re, down_im, preferred_element_type=jnp.float32)
        upd_re = (est_re.astype(jnp.float32) - step_size * (grad_re * norm)).astype(jnp.bfloat16)
        upd_im = (est_im.astype(jnp.float32) - step_size * (grad_im * norm)).astype(jnp.bfloat16)
        return (upd_re, upd_im)
    upd_re, upd_im = lax.map(per_freq, (estimate[0], estimate[1], data[0], data[1], window_data[0], window_data[1], wavelet.T))
    times = jnp.arange(NT, dtype=jnp.int32)
    phase = bins[:, None] * times[None, :] % NT
    angle = 2.0 * math.pi / NT * phase.astype(jnp.float32)
    table = jnp.concatenate([jnp.cos(angle), -jnp.sin(angle)], axis=0).astype(jnp.bfloat16)
    stacked = jnp.concatenate([upd_re, upd_im], axis=0).reshape(2 * NF, ROWS * RCV)
    trace = jnp.dot(table.T, stacked, preferred_element_type=jnp.float32) * math.sqrt(RCV / NF)
    trace = trace.reshape(NT, ROWS, RCV)
    level = threshold[0].astype(jnp.float32) / 64.0
    return (jnp.sign(trace) * jnp.maximum(jnp.abs(trace) - level, 0.0)).astype(jnp.bfloat16)
```

```python
from functools import partial
import math

import jax
import jax.numpy as jnp
from jax import lax
from jax.experimental import pallas as pl
from jax.experimental.pallas import tpu as pltpu
from jax.sharding import PartitionSpec as P

NF = 256
RCV = 4096
NT = 1024
FC = 8
MESH = pl.DeviceIdType.MESH


def iota(shape, dim):
    return lax.broadcasted_iota(jnp.int32, shape, dim)


def update_kernel(
    nx, nz, nchunk, rows, lines, norm,
    data, est, win, wav, pos, step, out,
    down, est_p, upd, mod_mine, mod_other,
    x_send, x_recv, c_send, c_recv, r_send, r_recv, l_send, l_recv, own_sem,
):
    mx = lax.axis_index("shot")
    mz = lax.axis_index("freq")
    mc = lax.axis_index("rcv")
    width = data.shape[2]
    fl = FC * lines
    fi = FC * rows

    barrier = pltpu.get_barrier_semaphore()
    for d in range(1, nx):
        pl.semaphore_signal(
            barrier, inc=1, device_id={"shot": lax.rem(mx + d, nx)}, device_id_type=MESH
        )
    pl.semaphore_signal(barrier, inc=1, device_id={"rcv": 1 - mc}, device_id_type=MESH)

    @pl.when(mz > 0)
    def _():
        pl.semaphore_signal(barrier, inc=1, device_id={"freq": mz - 1}, device_id_type=MESH)

    @pl.when(mz < nz - 1)
    def _():
        pl.semaphore_signal(barrier, inc=1, device_id={"freq": mz + 1}, device_id_type=MESH)

    ends = (mz > 0).astype(jnp.int32) + (mz < nz - 1).astype(jnp.int32)
    pl.semaphore_wait(barrier, nx + ends)

    def x_copy(d, k):
        piece = down.at[k, :, pl.ds(mx * fl, fl)]
        return pltpu.make_async_remote_copy(
            src_ref=piece, dst_ref=piece,
            send_sem=x_send.at[d, k], recv_sem=x_recv.at[d, k],
            device_id={"shot": lax.rem(mx + d, nx)}, device_id_type=MESH,
        )

    def c_copy(k):
        return pltpu.make_async_remote_copy(
            src_ref=mod_mine.at[k], dst_ref=mod_other.at[k],
            send_sem=c_send.at[k], recv_sem=c_recv.at[k],
            device_id={"rcv": 1 - mc}, device_id_type=MESH,
        )

    def z_copy(src, slot, k, way):
        send, recv = (r_send, r_recv) if way > 0 else (l_send, l_recv)
        return pltpu.make_async_remote_copy(
            src_ref=src, dst_ref=out.at[slot, k],
            send_sem=send.at[slot, k], recv_sem=recv.at[slot, k],
            device_id={"freq": mz + way}, device_id_type=MESH,
        )

    def own_copy(k):
        return pltpu.make_async_copy(upd.at[k], out.at[mz, k], own_sem.at[k])

    column = mc * width + iota((lines, width), 1)
    select = (column == pos[:, :]).astype(jnp.float32)

    def make_down(k, carry):
        for c in range(2):
            parts = []
            lines_k = data[c, pl.ds(pl.multiple_of(k * fl, fl), fl)].astype(jnp.float32)
            for f in range(FC):
                w = wav[c, k * FC + f]
                parts.append(w * select - lines_k[f * lines:(f + 1) * lines])
            down[k, c, pl.ds(pl.multiple_of(mx * fl, fl), fl)] = jnp.concatenate(
                parts, axis=0
            ).astype(jnp.bfloat16)
        for d in range(1, nx):
            x_copy(d, k).start()
        return carry

    lax.fori_loop(0, nchunk, make_down, 0)

    n = 2 * fi
    dst, src = iota((n, n), 0), iota((n, n), 1)
    want = (dst // FC % 2) * fi + (dst % FC) * rows + dst // (2 * FC)
    perm = (src == want).astype(jnp.bfloat16)

    def chunk_of(ref, k):
        part = pl.ds(pl.multiple_of(k * fi, fi), fi)
        return jnp.concatenate([ref[0, part], ref[1, part]], axis=0)

    def permute(k, carry):
        est_p[k] = jnp.dot(
            perm, chunk_of(est, k), preferred_element_type=jnp.float32
        ).astype(jnp.bfloat16)
        return carry

    lax.fori_loop(0, nchunk, permute, 0)

    cols = nx * fl
    shots = win.shape[2]
    s_row, s_col = iota((shots, cols), 0), iota((shots, cols), 1)
    spread = (s_row == (s_col // fl) * lines + s_col % lines).astype(jnp.bfloat16)
    shape3 = (rows, FC, cols)
    same = iota(shape3, 1) == iota(shape3, 2) % fl // lines
    scale = step[0]

    def model(k):
        for d in range(1, nx):
            here = down.at[k, :, pl.ds(lax.rem(mx + nx - d, nx) * fl, fl)]
            pltpu.make_async_remote_copy(
                src_ref=here, dst_ref=here,
                send_sem=x_send.at[d, k], recv_sem=x_recv.at[d, k],
                device_id={"shot": lax.rem(mx + d, nx)}, device_id_type=MESH,
            ).wait_recv()
        lines_k = down[k].reshape(2 * cols, width)
        m = lax.dot_general(
            est_p[k], lines_k, (((1,), (1,)), ((), ())), preferred_element_type=jnp.float32
        ).reshape(rows, 2, FC, 2 * cols)
        mod_mine[k, 0] = m[:, 0, :, :cols] - m[:, 1, :, cols:]
        mod_mine[k, 1] = m[:, 0, :, cols:] + m[:, 1, :, :cols]
        c_copy(k).start()

    def update(k):
        c_copy(k).wait_recv()
        total_re = mod_mine[k, 0] + mod_other[k, 0]
        total_im = mod_mine[k, 1] + mod_other[k, 1]
        w = jnp.dot(perm, chunk_of(win, k), preferred_element_type=jnp.float32).astype(jnp.bfloat16)
        w = jnp.dot(w, spread, preferred_element_type=jnp.float32).reshape(rows, 2, FC, cols)
        e_re = jnp.where(same, w[:, 0] - total_re, 0.0)
        e_im = jnp.where(same, w[:, 1] - total_im, 0.0)
        e = jnp.stack(
            [jnp.concatenate([e_re, e_im], axis=2), jnp.concatenate([e_im, -e_re], axis=2)], axis=1
        ).reshape(n, 2 * cols).astype(jnp.bfloat16)
        grad = jnp.dot(e, down[k].reshape(2 * cols, width), preferred_element_type=jnp.float32)
        upd[k] = (est_p[k].astype(jnp.float32) - scale * (grad * norm)).astype(jnp.bfloat16)
        own_copy(k).start()

        @pl.when(mz < nz - 1)
        def _():
            z_copy(upd.at[k], mz, k, 1).start()

        @pl.when(mz > 0)
        def _():
            z_copy(upd.at[k], mz, k, -1).start()

    def step_of(k, carry):
        @pl.when(k < nchunk)
        def _():
            model(k)

        @pl.when(k > 0)
        def _():
            update(k - 1)

        return carry

    lax.fori_loop(0, nchunk + 1, step_of, 0)

    def hop(h, carry):
        def one(k, carry):
            for way in (1, -1):
                slot = mz - way * h
                inside = (slot >= 0) & (slot < nz)
                more = (mz + way >= 0) & (mz + way < nz)

                @pl.when(inside)
                def _():
                    here = out.at[slot, k]
                    z_copy(here, slot, k, way).wait_recv()

                @pl.when(inside & more)
                def _():
                    z_copy(out.at[slot, k], slot, k, way).start()

            return carry

        return lax.fori_loop(0, nchunk, one, carry)

    lax.fori_loop(1, nz, hop, 0)

    def drain(k, carry):
        for d in range(1, nx):
            x_copy(d, k).wait_send()
        c_copy(k).wait_send()
        own_copy(k).wait()

        def hop_sent(h, carry):
            for way in (1, -1):
                slot = mz - way * h
                inside = (slot >= 0) & (slot < nz)
                more = (mz + way >= 0) & (mz + way < nz)

                @pl.when(inside & more)
                def _():
                    z_copy(upd.at[k], slot, k, way).wait_send()

            return carry

        return lax.fori_loop(0, nz, hop_sent, carry)

    lax.fori_loop(0, nchunk, drain, 0)


def trace_kernel(rows, t_group, gain, level, table, u, out, sparse):
    groups, _, width = u.shape
    part = 2 * FC
    nt = table.shape[0]
    lv = level[0]
    for i in range(rows):
        ui = u[:, i * part:(i + 1) * part, :].reshape(groups * part, width)
        tr = jnp.dot(table[...], ui, preferred_element_type=jnp.float32) * gain
        sparse[i] = (jnp.maximum(tr - lv, 0.0) + jnp.minimum(tr + lv, 0.0)).astype(jnp.bfloat16)
    n = t_group * rows
    dst, src = iota((n, n), 0), iota((n, n), 1)
    perm = (src == (dst % rows) * t_group + dst // rows).astype(jnp.bfloat16)
    for g in range(nt // t_group):
        x = sparse[:, g * t_group:(g + 1) * t_group, :].reshape(n, width)
        out[g * n:(g + 1) * n, :] = jnp.dot(
            perm, x, preferred_element_type=jnp.float32
        ).astype(jnp.bfloat16)


def body(nx, nz, data, estimate, window_data, wavelet, positions, bins, threshold, step):
    _, nf, lines, width = data.shape
    rows = estimate.shape[2]
    shots = window_data.shape[3]
    nchunk = nf // FC
    norm = 1.0 / math.sqrt(shots * RCV)
    fi, cols = FC * rows, nx * FC * lines
    vmem = pl.BlockSpec(memory_space=pltpu.VMEM)
    smem = pl.BlockSpec(memory_space=pltpu.SMEM)
    dma = pltpu.SemaphoreType.DMA
    spectra = pl.pallas_call(
        partial(update_kernel, nx, nz, nchunk, rows, lines, norm),
        out_shape=jax.ShapeDtypeStruct((nz, nchunk, 2 * fi, width), jnp.bfloat16),
        in_specs=[vmem, vmem, vmem, smem, vmem, smem],
        out_specs=pl.BlockSpec(memory_space=pl.ANY),
        scratch_shapes=[
            pltpu.VMEM((nchunk, 2, cols, width), jnp.bfloat16),
            pltpu.VMEM((nchunk, 2 * fi, width), jnp.bfloat16),
            pltpu.VMEM((nchunk, 2 * fi, width), jnp.bfloat16),
            pltpu.VMEM((nchunk, 2, rows, FC, cols), jnp.float32),
            pltpu.VMEM((nchunk, 2, rows, FC, cols), jnp.float32),
            dma((nx, nchunk)), dma((nx, nchunk)),
            dma((nchunk,)), dma((nchunk,)),
            dma((nz, nchunk)), dma((nz, nchunk)),
            dma((nz, nchunk)), dma((nz, nchunk)),
            dma((nchunk,)),
        ],
        compiler_params=pltpu.CompilerParams(
            collective_id=0, has_side_effects=True, vmem_limit_bytes=56 << 20
        ),
        name="update",
    )(
        data.reshape(2, nf * lines, width),
        estimate.reshape(2, nf * rows, width),
        window_data.reshape(2, nf * rows, shots),
        wavelet,
        positions[:, None],
        step,
    )
    nt = NT // nz
    times = lax.axis_index("freq") * nt + lax.iota(jnp.int32, nt)
    phase = times[:, None] * bins[None, :] % NT
    angle = 2.0 * math.pi / NT * phase.astype(jnp.float32)
    table = jnp.stack([jnp.cos(angle), -jnp.sin(angle)], axis=1).astype(jnp.bfloat16)
    table = table.reshape(nt, 2, nz * nchunk, FC).transpose(0, 2, 1, 3).reshape(nt, 2 * nz * nf)
    level = threshold.astype(jnp.float32) / 64.0
    block = 256
    groups = nz * nchunk
    traces = pl.pallas_call(
        partial(trace_kernel, rows, 32, math.sqrt(RCV / NF)),
        out_shape=jax.ShapeDtypeStruct((nt * rows, width), jnp.bfloat16),
        grid=(width // block,),
        in_specs=[
            smem,
            pl.BlockSpec((nt, 2 * nz * nf), lambda j: (0, 0)),
            pl.BlockSpec((groups, 2 * fi, block), lambda j: (0, 0, j)),
        ],
        out_specs=pl.BlockSpec((nt * rows, block), lambda j: (0, j)),
        scratch_shapes=[pltpu.VMEM((rows, nt, block), jnp.bfloat16)],
        compiler_params=pltpu.CompilerParams(vmem_limit_bytes=40 << 20),
        name="traces",
    )(level, table, spectra.reshape(groups, 2 * fi, width))
    return traces.reshape(nt, rows, width)


def solution(mesh):
    return jax.shard_map(
        partial(body, mesh.shape["shot"], mesh.shape["freq"]),
        mesh=mesh,
        in_specs=(
            P(None, "freq", ("grp", "shot"), "rcv"),
            P(None, "freq", ("grp", "shot"), "rcv"),
            P(None, "freq", ("grp", "shot"), None),
            P(None, ("grp", "freq")),
            P(("grp", "shot")),
            P("grp"),
            P("grp"),
            P("grp"),
        ),
        out_specs=P("freq", ("grp", "shot"), "rcv"),
        check_vma=False,
    )
```

```python
from functools import partial
import math

import jax
import jax.numpy as jnp
from jax import lax
from jax.experimental import pallas as pl
from jax.experimental.pallas import tpu as pltpu
from jax.sharding import PartitionSpec as P

NF = 256
RCV = 4096
NT = 1024
FC = 8
BLOCK = 256
LAG = 2
MESH = pl.DeviceIdType.MESH


def iota(shape, dim):
    return lax.broadcasted_iota(jnp.int32, shape, dim)


def make_traces(u, table, lv, gain, rows, t_group, sparse, out):
    groups, _, width = u.shape
    part = 2 * FC
    nt = table.shape[0]
    for i in range(rows):
        ui = u[:, i * part:(i + 1) * part, :].reshape(groups * part, width)
        tr = jnp.dot(table[...], ui, preferred_element_type=jnp.float32) * gain
        sparse[i] = (jnp.maximum(tr - lv, 0.0) + jnp.minimum(tr + lv, 0.0)).astype(jnp.bfloat16)
    n = t_group * rows
    dst, src = iota((n, n), 0), iota((n, n), 1)
    perm = (src == (dst % rows) * t_group + dst // rows).astype(jnp.bfloat16)
    for g in range(nt // t_group):
        x = sparse[:, g * t_group:(g + 1) * t_group, :].reshape(n, width)
        out[g * n:(g + 1) * n, :] = jnp.dot(
            perm, x, preferred_element_type=jnp.float32
        ).astype(jnp.bfloat16)


def update_kernel(
    nx, nz, nchunk, rows, lines, norm, blocks, helped, gain, t_group,
    data, est, win, wav, pos, step, level, table, out, given,
    down, est_p, upd, mod_mine, mod_other, ubuf, sparse, made,
    x_send, x_recv, c_send, c_recv, za_send, za_recv, zb_send, zb_recv,
    zc_send, zc_recv, g_send, g_recv, own_sem, ubuf_sem,
):
    mx = lax.axis_index("shot")
    mz = lax.axis_index("freq")
    mc = lax.axis_index("rcv")
    width = data.shape[2]
    fl = FC * lines
    fi = FC * rows

    barrier = pltpu.get_barrier_semaphore()
    for d in range(1, nx):
        pl.semaphore_signal(
            barrier, inc=1, device_id={"shot": lax.rem(mx + d, nx)}, device_id_type=MESH
        )
    pl.semaphore_signal(barrier, inc=1, device_id={"rcv": 1 - mc}, device_id_type=MESH)

    @pl.when(mz > 0)
    def _():
        pl.semaphore_signal(barrier, inc=1, device_id={"freq": mz - 1}, device_id_type=MESH)

    @pl.when(mz < nz - 1)
    def _():
        pl.semaphore_signal(barrier, inc=1, device_id={"freq": mz + 1}, device_id_type=MESH)

    ends = (mz > 0).astype(jnp.int32) + (mz < nz - 1).astype(jnp.int32)
    pl.semaphore_wait(barrier, nx + ends)

    def x_copy(d, k):
        piece = down.at[k, :, pl.ds(mx * fl, fl)]
        return pltpu.make_async_remote_copy(
            src_ref=piece, dst_ref=piece,
            send_sem=x_send.at[d, k], recv_sem=x_recv.at[d, k],
            device_id={"shot": lax.rem(mx + d, nx)}, device_id_type=MESH,
        )

    def c_copy(k):
        return pltpu.make_async_remote_copy(
            src_ref=mod_mine.at[k], dst_ref=mod_other.at[k],
            send_sem=c_send.at[k], recv_sem=c_recv.at[k],
            device_id={"rcv": 1 - mc}, device_id_type=MESH,
        )

    def w_of(way):
        return 0 if way > 0 else 1

    def last(z, way):
        return z == (nz - 1 if way > 0 else 0)

    def a_copy(src, slot, k, way):
        return pltpu.make_async_remote_copy(
            src_ref=src, dst_ref=out.at[pl.ds(0, helped), slot, k],
            send_sem=za_send.at[w_of(way), slot, k], recv_sem=za_recv.at[w_of(way), slot, k],
            device_id={"freq": mz + way}, device_id_type=MESH,
        )

    def b_copy(src, slot, k, way):
        return pltpu.make_async_remote_copy(
            src_ref=src, dst_ref=out.at[pl.ds(helped, blocks - helped), slot, k],
            send_sem=zb_send.at[w_of(way), slot, k], recv_sem=zb_recv.at[w_of(way), slot, k],
            device_id={"freq": mz + way}, device_id_type=MESH,
        )

    def block_copy(slot, b, way):
        piece = out.at[b, slot]
        return pltpu.make_async_remote_copy(
            src_ref=piece, dst_ref=piece,
            send_sem=zc_send.at[w_of(way), slot, b], recv_sem=zc_recv.at[w_of(way), slot, b],
            device_id={"freq": mz + way}, device_id_type=MESH,
        )

    def given_copy(b, way):
        return pltpu.make_async_remote_copy(
            src_ref=made.at[b], dst_ref=given.at[b],
            send_sem=g_send.at[b], recv_sem=g_recv.at[b],
            device_id={"freq": mz + way}, device_id_type=MESH,
        )

    a_own = lambda k: upd.at[k, pl.ds(0, helped)]
    b_own = lambda k: upd.at[k, pl.ds(helped, blocks - helped)]
    a_out = lambda slot, k: out.at[pl.ds(0, helped), slot, k]
    b_out = lambda slot, k: out.at[pl.ds(helped, blocks - helped), slot, k]

    def own_copy(k):
        return pltpu.make_async_copy(upd.at[k], out.at[:, mz, k], own_sem.at[k])

    column = mc * width + iota((lines, width), 1)
    select = (column == pos[:, :]).astype(jnp.float32)

    def make_down(k, carry):
        for c in range(2):
            parts = []
            lines_k = data[c, pl.ds(pl.multiple_of(k * fl, fl), fl)].astype(jnp.float32)
            for f in range(FC):
                w = wav[c, k * FC + f]
                parts.append(w * select - lines_k[f * lines:(f + 1) * lines])
            down[k, c, pl.ds(pl.multiple_of(mx * fl, fl), fl)] = jnp.concatenate(
                parts, axis=0
            ).astype(jnp.bfloat16)
        for d in range(1, nx):
            x_copy(d, k).start()
        return carry

    lax.fori_loop(0, nchunk, make_down, 0)

    n = 2 * fi
    dst, src = iota((n, n), 0), iota((n, n), 1)
    want = (dst // FC % 2) * fi + (dst % FC) * rows + dst // (2 * FC)
    perm = (src == want).astype(jnp.bfloat16)

    def chunk_of(ref, k):
        part = pl.ds(pl.multiple_of(k * fi, fi), fi)
        return jnp.concatenate([ref[0, part], ref[1, part]], axis=0)

    def permute(k, carry):
        est_p[k] = jnp.dot(
            perm, chunk_of(est, k), preferred_element_type=jnp.float32
        ).astype(jnp.bfloat16)
        return carry

    lax.fori_loop(0, nchunk, permute, 0)

    cols = nx * fl
    shots = win.shape[2]
    s_row, s_col = iota((shots, cols), 0), iota((shots, cols), 1)
    spread = (s_row == (s_col // fl) * lines + s_col % lines).astype(jnp.bfloat16)
    shape3 = (rows, FC, cols)
    same = iota(shape3, 1) == iota(shape3, 2) % fl // lines
    scale = step[0]

    def model(k):
        for d in range(1, nx):
            here = down.at[k, :, pl.ds(lax.rem(mx + nx - d, nx) * fl, fl)]
            pltpu.make_async_remote_copy(
                src_ref=here, dst_ref=here,
                send_sem=x_send.at[d, k], recv_sem=x_recv.at[d, k],
                device_id={"shot": lax.rem(mx + d, nx)}, device_id_type=MESH,
            ).wait_recv()
        lines_k = down[k].reshape(2 * cols, width)
        m = lax.dot_general(
            est_p[k], lines_k, (((1,), (1,)), ((), ())), preferred_element_type=jnp.float32
        ).reshape(rows, 2, FC, 2 * cols)
        mod_mine[k, 0] = m[:, 0, :, :cols] - m[:, 1, :, cols:]
        mod_mine[k, 1] = m[:, 0, :, cols:] + m[:, 1, :, :cols]
        c_copy(k).start()

    def update(k):
        c_copy(k).wait_recv()
        total_re = mod_mine[k, 0] + mod_other[k, 0]
        total_im = mod_mine[k, 1] + mod_other[k, 1]
        w = jnp.dot(perm, chunk_of(win, k), preferred_element_type=jnp.float32).astype(jnp.bfloat16)
        w = jnp.dot(w, spread, preferred_element_type=jnp.float32).reshape(rows, 2, FC, cols)
        e_re = jnp.where(same, w[:, 0] - total_re, 0.0)
        e_im = jnp.where(same, w[:, 1] - total_im, 0.0)
        e = jnp.stack(
            [jnp.concatenate([e_re, e_im], axis=2), jnp.concatenate([e_im, -e_re], axis=2)], axis=1
        ).reshape(n, 2 * cols).astype(jnp.bfloat16)
        grad = jnp.dot(e, down[k].reshape(2 * cols, width), preferred_element_type=jnp.float32)
        new = (est_p[k].astype(jnp.float32) - scale * (grad * norm)).astype(jnp.bfloat16)
        for b in range(blocks):
            upd[k, b] = new[:, b * BLOCK:(b + 1) * BLOCK]
        own_copy(k).start()
        for way in (1, -1):
            @pl.when(jnp.logical_not(last(mz, way)))
            def _():
                b_copy(b_own(k), mz, k, way).start()

                if helped:
                    @pl.when(jnp.logical_not(last(mz + way, way)))
                    def _():
                        a_copy(a_own(k), mz, k, way).start()

    def near(k):
        for way in (1, -1):
            slot = mz - way

            @pl.when((slot >= 0) & (slot < nz))
            def _():
                b_copy(b_out(slot, k), slot, k, way).wait_recv()

                if helped:
                    @pl.when(jnp.logical_not(last(mz, way)))
                    def _():
                        a_copy(a_out(slot, k), slot, k, way).wait_recv()

                @pl.when(last(mz + way, way))
                def _():
                    b_copy(b_out(slot, k), slot, k, way).start()

    def step_of(k, carry):
        @pl.when(k < nchunk)
        def _():
            model(k)

        @pl.when((k > 0) & (k <= nchunk))
        def _():
            update(k - 1)

        @pl.when(k >= LAG)
        def _():
            near(k - LAG)

        return carry

    lax.fori_loop(0, nchunk + LAG, step_of, 0)

    def own_done(k, carry):
        own_copy(k).wait()
        return carry

    lax.fori_loop(0, nchunk, own_done, 0)

    def hand_on(b, carry):
        for way in (1, -1):
            slot = mz - way
            inside = (slot >= 0) & (slot < nz)
            nxt = mz + way

            @pl.when(inside & (nxt > 0) & (nxt < nz - 1))
            def _():
                block_copy(slot, b, way).start()

        return carry

    lax.fori_loop(0, blocks, hand_on, 0)

    def far(h, carry):
        def one(b, carry):
            for way in (1, -1):
                slot = mz - way * h
                nxt = mz + way
                inside = (slot >= 0) & (slot < nz)
                at_end = last(mz, way)

                @pl.when(inside & jnp.logical_not(at_end))
                def _():
                    block_copy(slot, b, way).wait_recv()

                    @pl.when(jnp.logical_not(last(nxt, way)) | (b >= helped))
                    def _():
                        block_copy(slot, b, way).start()

                    if helped:
                        @pl.when(last(nxt, way) & (b < helped) & last(slot, -way))
                        def _():
                            load = pltpu.make_async_copy(out.at[b], ubuf, ubuf_sem)
                            load.start()
                            load.wait()
                            make_traces(
                                ubuf.reshape(nz * nchunk, ubuf.shape[2], BLOCK), table, level[0],
                                gain, rows, t_group, sparse, made.at[b],
                            )
                            given_copy(b, way).start()

                @pl.when(inside & at_end & (b >= helped))
                def _():
                    if not near_by:
                        block_copy(slot, b, way).wait_recv()

            return carry

        near_by = isinstance(h, int)
        return lax.fori_loop(0, blocks, one, carry)

    def end_chunk(k, carry):
        for way in (1, -1):
            slot = mz - 2 * way

            @pl.when((slot >= 0) & (slot < nz) & last(mz, way))
            def _():
                b_copy(b_out(slot, k), slot, k, way).wait_recv()

        return carry

    if nz > 2:
        lax.fori_loop(0, nchunk, end_chunk, 0)
        far(2, 0)
    lax.fori_loop(3, nz, far, 0)

    if helped:
        def take(b, carry):
            for way in (1, -1):
                @pl.when(last(mz, way))
                def _():
                    given_copy(b, way).wait_recv()

                @pl.when(last(mz + way, way))
                def _():
                    given_copy(b, way).wait_send()

            return carry

        lax.fori_loop(0, helped, take, 0)

    def drain(k, carry):
        for d in range(1, nx):
            x_copy(d, k).wait_send()
        c_copy(k).wait_send()
        for way in (1, -1):
            nxt = mz + way

            @pl.when(jnp.logical_not(last(mz, way)))
            def _():
                b_copy(b_own(k), mz, k, way).wait_send()

                if helped:
                    @pl.when(jnp.logical_not(last(nxt, way)))
                    def _():
                        a_copy(a_own(k), mz, k, way).wait_send()

            slot = mz - way

            @pl.when((slot >= 0) & (slot < nz) & last(nxt, way))
            def _():
                b_copy(b_own(k), slot, k, way).wait_send()

        return carry

    lax.fori_loop(0, nchunk, drain, 0)

    def drain_far(h, carry):
        def one(b, carry):
            for way in (1, -1):
                slot = mz - way * h
                nxt = mz + way
                inside = (slot >= 0) & (slot < nz) & (nxt >= 0) & (nxt < nz)
                to_end = last(nxt, way)

                @pl.when(inside & (jnp.logical_not(to_end) | ((b >= helped) & (h > 1))))
                def _():
                    block_copy(slot, b, way).wait_send()

            return carry

        return lax.fori_loop(0, blocks, one, carry)

    lax.fori_loop(1, nz, drain_far, 0)


def trace_kernel(rows, t_group, gain, helped, level, taken, table, u, given, out, sparse):
    ready = (pl.program_id(0) < helped) & (taken[0] > 0)

    @pl.when(ready)
    def _():
        out[...] = given[...]

    @pl.when(jnp.logical_not(ready))
    def _():
        make_traces(u, table, level[0], gain, rows, t_group, sparse, out)


def body(nx, nz, data, estimate, window_data, wavelet, positions, bins, threshold, step):
    _, nf, lines, width = data.shape
    rows = estimate.shape[2]
    shots = window_data.shape[3]
    nchunk = nf // FC
    norm = 1.0 / math.sqrt(shots * RCV)
    fi, cols = FC * rows, nx * FC * lines
    mz = lax.axis_index("freq")
    nt = NT // nz
    blocks, groups = width // BLOCK, nz * nchunk
    helped = blocks // 2 if nz >= 4 else 0
    held = max(helped, 1)
    gain, t_group = math.sqrt(RCV / NF), 32
    level = threshold.astype(jnp.float32) / 64.0

    def table_of(z):
        times = z * nt + lax.iota(jnp.int32, nt)
        phase = times[:, None] * bins[None, :] % NT
        angle = 2.0 * math.pi / NT * phase.astype(jnp.float32)
        table = jnp.stack([jnp.cos(angle), -jnp.sin(angle)], axis=1).astype(jnp.bfloat16)
        table = table.reshape(nt, 2, groups, FC).transpose(0, 2, 1, 3)
        return table.reshape(nt, 2 * nz * nf)

    vmem = pl.BlockSpec(memory_space=pltpu.VMEM)
    smem = pl.BlockSpec(memory_space=pltpu.SMEM)
    hbm = pl.BlockSpec(memory_space=pl.ANY)
    dma = pltpu.SemaphoreType.DMA
    spectra, given = pl.pallas_call(
        partial(
            update_kernel, nx, nz, nchunk, rows, lines, norm, blocks, helped, gain, t_group
        ),
        out_shape=(
            jax.ShapeDtypeStruct((blocks, nz, nchunk, 2 * fi, BLOCK), jnp.bfloat16),
            jax.ShapeDtypeStruct((held, nt * rows, BLOCK), jnp.bfloat16),
        ),
        in_specs=[vmem, vmem, vmem, smem, vmem, smem, smem, vmem],
        out_specs=(hbm, hbm),
        scratch_shapes=[
            pltpu.VMEM((nchunk, 2, cols, width), jnp.bfloat16),
            pltpu.VMEM((nchunk, 2 * fi, width), jnp.bfloat16),
            pltpu.VMEM((nchunk, blocks, 2 * fi, BLOCK), jnp.bfloat16),
            pltpu.VMEM((nchunk, 2, rows, FC, cols), jnp.float32),
            pltpu.VMEM((nchunk, 2, rows, FC, cols), jnp.float32),
            pltpu.VMEM((nz, nchunk, 2 * fi, BLOCK), jnp.bfloat16),
            pltpu.VMEM((rows, nt, BLOCK), jnp.bfloat16),
            pltpu.VMEM((held, nt * rows, BLOCK), jnp.bfloat16),
            dma((nx, nchunk)), dma((nx, nchunk)),
            dma((nchunk,)), dma((nchunk,)),
            dma((2, nz, nchunk)), dma((2, nz, nchunk)),
            dma((2, nz, nchunk)), dma((2, nz, nchunk)),
            dma((2, nz, blocks)), dma((2, nz, blocks)),
            dma((held,)), dma((held,)),
            dma((nchunk,)), dma,
        ],
        compiler_params=pltpu.CompilerParams(
            collective_id=0, has_side_effects=True, vmem_limit_bytes=58 << 20
        ),
        name="update",
    )(
        data.reshape(2, nf * lines, width),
        estimate.reshape(2, nf * rows, width),
        window_data.reshape(2, nf * rows, shots),
        wavelet,
        positions[:, None],
        step,
        level,
        table_of(jnp.where(mz < nz // 2, 0, nz - 1)),
    )
    taken = ((mz == 0) | (mz == nz - 1)).astype(jnp.int32)[None]
    traces = pl.pallas_call(
        partial(trace_kernel, rows, t_group, gain, helped),
        out_shape=jax.ShapeDtypeStruct((nt * rows, width), jnp.bfloat16),
        grid=(blocks,),
        in_specs=[
            smem,
            smem,
            pl.BlockSpec((nt, 2 * nz * nf), lambda j: (0, 0)),
            pl.BlockSpec((None, groups, 2 * fi, BLOCK), lambda j: (j, 0, 0, 0)),
            pl.BlockSpec(
                (None, nt * rows, BLOCK), lambda j: (jnp.minimum(j, held - 1), 0, 0)
            ),
        ],
        out_specs=pl.BlockSpec((nt * rows, BLOCK), lambda j: (0, j)),
        scratch_shapes=[pltpu.VMEM((rows, nt, BLOCK), jnp.bfloat16)],
        compiler_params=pltpu.CompilerParams(vmem_limit_bytes=40 << 20),
        name="traces",
    )(level, taken, table_of(mz), spectra.reshape(blocks, groups, 2 * fi, BLOCK), given)
    return traces.reshape(nt, rows, width)


def solution(mesh):
    return jax.shard_map(
        partial(body, mesh.shape["shot"], mesh.shape["freq"]),
        mesh=mesh,
        in_specs=(
            P(None, "freq", ("grp", "shot"), "rcv"),
            P(None, "freq", ("grp", "shot"), "rcv"),
            P(None, "freq", ("grp", "shot"), None),
            P(None, ("grp", "freq")),
            P(("grp", "shot")),
            P("grp"),
            P("grp"),
            P("grp"),
        ),
        out_specs=P("freq", ("grp", "shot"), "rcv"),
        check_vma=False,
    )
```

```python
from functools import partial
import math

import jax
import jax.numpy as jnp
from jax import lax
from jax.experimental import pallas as pl
from jax.experimental.pallas import tpu as pltpu
from jax.sharding import PartitionSpec as P

NF = 256
RCV = 4096
NT = 1024
FC = 8
BLOCK = 256
LAG = 1
MESH = pl.DeviceIdType.MESH


def iota(shape, dim):
    return lax.broadcasted_iota(jnp.int32, shape, dim)


def make_traces(u, table, lv, gain, rows, t_group, sparse, out):
    groups, _, width = u.shape
    part = 2 * FC
    nt = table.shape[0]
    for i in range(rows):
        ui = u[:, i * part:(i + 1) * part, :].reshape(groups * part, width)
        tr = jnp.dot(table[...], ui, preferred_element_type=jnp.float32) * gain
        sparse[i] = (jnp.maximum(tr - lv, 0.0) + jnp.minimum(tr + lv, 0.0)).astype(jnp.bfloat16)
    n = t_group * rows
    dst, src = iota((n, n), 0), iota((n, n), 1)
    perm = (src == (dst % rows) * t_group + dst // rows).astype(jnp.bfloat16)
    for g in range(nt // t_group):
        x = sparse[:, g * t_group:(g + 1) * t_group, :].reshape(n, width)
        out[g * n:(g + 1) * n, :] = jnp.dot(
            perm, x, preferred_element_type=jnp.float32
        ).astype(jnp.bfloat16)


def update_kernel(
    nx, nz, nchunk, rows, lines, norm, blocks, helped, gain, t_group,
    data, est, win, wav, pos, step, level, table, out, given,
    down, est_p, upd, mod_mine, mod_other, ubuf, sparse, made,
    x_send, x_recv, c_send, c_recv, za_send, za_recv, zb_send, zb_recv,
    zc_send, zc_recv, g_send, g_recv, own_sem, ubuf_sem,
):
    mx = lax.axis_index("shot")
    mz = lax.axis_index("freq")
    mc = lax.axis_index("rcv")
    width = data.shape[2]
    fl = FC * lines
    fi = FC * rows

    barrier = pltpu.get_barrier_semaphore()
    for d in range(1, nx):
        pl.semaphore_signal(
            barrier, inc=1, device_id={"shot": lax.rem(mx + d, nx)}, device_id_type=MESH
        )
    pl.semaphore_signal(barrier, inc=1, device_id={"rcv": 1 - mc}, device_id_type=MESH)

    @pl.when(mz > 0)
    def _():
        pl.semaphore_signal(barrier, inc=1, device_id={"freq": mz - 1}, device_id_type=MESH)

    @pl.when(mz < nz - 1)
    def _():
        pl.semaphore_signal(barrier, inc=1, device_id={"freq": mz + 1}, device_id_type=MESH)

    ends = (mz > 0).astype(jnp.int32) + (mz < nz - 1).astype(jnp.int32)
    pl.semaphore_wait(barrier, nx + ends)

    def x_copy(d, k):
        piece = down.at[k, :, pl.ds(mx * fl, fl)]
        return pltpu.make_async_remote_copy(
            src_ref=piece, dst_ref=piece,
            send_sem=x_send.at[d, k], recv_sem=x_recv.at[d, k],
            device_id={"shot": lax.rem(mx + d, nx)}, device_id_type=MESH,
        )

    def c_copy(k):
        return pltpu.make_async_remote_copy(
            src_ref=mod_mine.at[k], dst_ref=mod_other.at[k],
            send_sem=c_send.at[k], recv_sem=c_recv.at[k],
            device_id={"rcv": 1 - mc}, device_id_type=MESH,
        )

    def w_of(way):
        return 0 if way > 0 else 1

    def last(z, way):
        return z == (nz - 1 if way > 0 else 0)

    def a_copy(src, slot, k, way):
        return pltpu.make_async_remote_copy(
            src_ref=src, dst_ref=out.at[pl.ds(0, helped), slot, k],
            send_sem=za_send.at[w_of(way), slot, k], recv_sem=za_recv.at[w_of(way), slot, k],
            device_id={"freq": mz + way}, device_id_type=MESH,
        )

    def b_copy(src, slot, k, way):
        return pltpu.make_async_remote_copy(
            src_ref=src, dst_ref=out.at[pl.ds(helped, blocks - helped), slot, k],
            send_sem=zb_send.at[w_of(way), slot, k], recv_sem=zb_recv.at[w_of(way), slot, k],
            device_id={"freq": mz + way}, device_id_type=MESH,
        )

    def block_copy(slot, b, way):
        piece = out.at[b, slot]
        return pltpu.make_async_remote_copy(
            src_ref=piece, dst_ref=piece,
            send_sem=zc_send.at[w_of(way), slot, b], recv_sem=zc_recv.at[w_of(way), slot, b],
            device_id={"freq": mz + way}, device_id_type=MESH,
        )

    def given_copy(b, way):
        return pltpu.make_async_remote_copy(
            src_ref=made.at[b], dst_ref=given.at[b],
            send_sem=g_send.at[b], recv_sem=g_recv.at[b],
            device_id={"freq": mz + way}, device_id_type=MESH,
        )

    a_own = lambda k: upd.at[k, pl.ds(0, helped)]
    b_own = lambda k: upd.at[k, pl.ds(helped, blocks - helped)]
    a_out = lambda slot, k: out.at[pl.ds(0, helped), slot, k]
    b_out = lambda slot, k: out.at[pl.ds(helped, blocks - helped), slot, k]

    def own_copy(k):
        return pltpu.make_async_copy(upd.at[k], out.at[:, mz, k], own_sem.at[k])

    column = mc * width + iota((lines, width), 1)
    select = (column == pos[:, :]).astype(jnp.float32)

    def make_down(k, carry):
        for c in range(2):
            parts = []
            lines_k = data[c, pl.ds(pl.multiple_of(k * fl, fl), fl)].astype(jnp.float32)
            for f in range(FC):
                w = wav[c, k * FC + f]
                parts.append(w * select - lines_k[f * lines:(f + 1) * lines])
            down[k, c, pl.ds(pl.multiple_of(mx * fl, fl), fl)] = jnp.concatenate(
                parts, axis=0
            ).astype(jnp.bfloat16)
        for d in range(1, nx):
            x_copy(d, k).start()
        return carry

    lax.fori_loop(0, nchunk, make_down, 0)

    n = 2 * fi
    dst, src = iota((n, n), 0), iota((n, n), 1)
    want = (dst // FC % 2) * fi + (dst % FC) * rows + dst // (2 * FC)
    perm = (src == want).astype(jnp.bfloat16)

    def chunk_of(ref, k):
        part = pl.ds(pl.multiple_of(k * fi, fi), fi)
        return jnp.concatenate([ref[0, part], ref[1, part]], axis=0)

    def permute(k, carry):
        est_p[k] = jnp.dot(
            perm, chunk_of(est, k), preferred_element_type=jnp.float32
        ).astype(jnp.bfloat16)
        return carry

    lax.fori_loop(0, nchunk, permute, 0)

    cols = nx * fl
    shots = win.shape[2]
    s_row, s_col = iota((shots, cols), 0), iota((shots, cols), 1)
    spread = (s_row == (s_col // fl) * lines + s_col % lines).astype(jnp.bfloat16)
    shape3 = (rows, FC, cols)
    same = iota(shape3, 1) == iota(shape3, 2) % fl // lines
    scale = step[0]

    def model(k):
        for d in range(1, nx):
            here = down.at[k, :, pl.ds(lax.rem(mx + nx - d, nx) * fl, fl)]
            pltpu.make_async_remote_copy(
                src_ref=here, dst_ref=here,
                send_sem=x_send.at[d, k], recv_sem=x_recv.at[d, k],
                device_id={"shot": lax.rem(mx + d, nx)}, device_id_type=MESH,
            ).wait_recv()
        lines_k = down[k].reshape(2 * cols, width)
        m = lax.dot_general(
            est_p[k], lines_k, (((1,), (1,)), ((), ())), preferred_element_type=jnp.float32
        ).reshape(rows, 2, FC, 2 * cols)
        mod_mine[k, 0] = m[:, 0, :, :cols] - m[:, 1, :, cols:]
        mod_mine[k, 1] = m[:, 0, :, cols:] + m[:, 1, :, :cols]
        c_copy(k).start()

    def update(k):
        c_copy(k).wait_recv()
        total_re = mod_mine[k, 0] + mod_other[k, 0]
        total_im = mod_mine[k, 1] + mod_other[k, 1]
        w = jnp.dot(perm, chunk_of(win, k), preferred_element_type=jnp.float32).astype(jnp.bfloat16)
        w = jnp.dot(w, spread, preferred_element_type=jnp.float32).reshape(rows, 2, FC, cols)
        e_re = jnp.where(same, w[:, 0] - total_re, 0.0)
        e_im = jnp.where(same, w[:, 1] - total_im, 0.0)
        e = jnp.stack(
            [jnp.concatenate([e_re, e_im], axis=2), jnp.concatenate([e_im, -e_re], axis=2)], axis=1
        ).reshape(n, 2 * cols).astype(jnp.bfloat16)
        grad = jnp.dot(e, down[k].reshape(2 * cols, width), preferred_element_type=jnp.float32)
        new = (est_p[k].astype(jnp.float32) - scale * (grad * norm)).astype(jnp.bfloat16)
        for b in range(blocks):
            upd[k, b] = new[:, b * BLOCK:(b + 1) * BLOCK]
        own_copy(k).start()
        for way in (1, -1):
            @pl.when(jnp.logical_not(last(mz, way)))
            def _():
                b_copy(b_own(k), mz, k, way).start()

                if helped:
                    @pl.when(jnp.logical_not(last(mz + way, way)))
                    def _():
                        a_copy(a_own(k), mz, k, way).start()

    def near(k):
        for way in (1, -1):
            slot = mz - way

            @pl.when((slot >= 0) & (slot < nz))
            def _():
                b_copy(b_out(slot, k), slot, k, way).wait_recv()

                if helped:
                    @pl.when(jnp.logical_not(last(mz, way)))
                    def _():
                        a_copy(a_out(slot, k), slot, k, way).wait_recv()

                @pl.when(last(mz + way, way))
                def _():
                    b_copy(b_out(slot, k), slot, k, way).start()

    def step_of(k, carry):
        @pl.when(k < nchunk)
        def _():
            model(k)
            update(k)

        @pl.when(k >= LAG)
        def _():
            near(k - LAG)

        return carry

    lax.fori_loop(0, nchunk + LAG, step_of, 0)

    def own_done(k, carry):
        own_copy(k).wait()
        return carry

    lax.fori_loop(0, nchunk, own_done, 0)

    def hand_on(b, carry):
        for way in (1, -1):
            slot = mz - way
            inside = (slot >= 0) & (slot < nz)
            nxt = mz + way

            @pl.when(inside & (nxt > 0) & (nxt < nz - 1))
            def _():
                block_copy(slot, b, way).start()

        return carry

    lax.fori_loop(0, blocks, hand_on, 0)

    def far(h, carry):
        def one(b, carry):
            for way in (1, -1):
                slot = mz - way * h
                nxt = mz + way
                inside = (slot >= 0) & (slot < nz)
                at_end = last(mz, way)

                @pl.when(inside & jnp.logical_not(at_end))
                def _():
                    block_copy(slot, b, way).wait_recv()

                    @pl.when(jnp.logical_not(last(nxt, way)) | (b >= helped))
                    def _():
                        block_copy(slot, b, way).start()

                    if helped:
                        @pl.when(last(nxt, way) & (b < helped) & last(slot, -way))
                        def _():
                            load = pltpu.make_async_copy(out.at[b], ubuf, ubuf_sem)
                            load.start()
                            load.wait()
                            make_traces(
                                ubuf.reshape(nz * nchunk, ubuf.shape[2], BLOCK), table, level[0],
                                gain, rows, t_group, sparse, made.at[b],
                            )
                            given_copy(b, way).start()

                @pl.when(inside & at_end & (b >= helped))
                def _():
                    if not near_by:
                        block_copy(slot, b, way).wait_recv()

            return carry

        near_by = isinstance(h, int)
        return lax.fori_loop(0, blocks, one, carry)

    def end_chunk(k, carry):
        for way in (1, -1):
            slot = mz - 2 * way

            @pl.when((slot >= 0) & (slot < nz) & last(mz, way))
            def _():
                b_copy(b_out(slot, k), slot, k, way).wait_recv()

        return carry

    if nz > 2:
        lax.fori_loop(0, nchunk, end_chunk, 0)
        far(2, 0)
    lax.fori_loop(3, nz, far, 0)

    if helped:
        def take(b, carry):
            for way in (1, -1):
                @pl.when(last(mz, way))
                def _():
                    given_copy(b, way).wait_recv()

                @pl.when(last(mz + way, way))
                def _():
                    given_copy(b, way).wait_send()

            return carry

        lax.fori_loop(0, helped, take, 0)

    def drain(k, carry):
        for d in range(1, nx):
            x_copy(d, k).wait_send()
        c_copy(k).wait_send()
        for way in (1, -1):
            nxt = mz + way

            @pl.when(jnp.logical_not(last(mz, way)))
            def _():
                b_copy(b_own(k), mz, k, way).wait_send()

                if helped:
                    @pl.when(jnp.logical_not(last(nxt, way)))
                    def _():
                        a_copy(a_own(k), mz, k, way).wait_send()

            slot = mz - way

            @pl.when((slot >= 0) & (slot < nz) & last(nxt, way))
            def _():
                b_copy(b_own(k), slot, k, way).wait_send()

        return carry

    lax.fori_loop(0, nchunk, drain, 0)

    def drain_far(h, carry):
        def one(b, carry):
            for way in (1, -1):
                slot = mz - way * h
                nxt = mz + way
                inside = (slot >= 0) & (slot < nz) & (nxt >= 0) & (nxt < nz)
                to_end = last(nxt, way)

                @pl.when(inside & (jnp.logical_not(to_end) | ((b >= helped) & (h > 1))))
                def _():
                    block_copy(slot, b, way).wait_send()

            return carry

        return lax.fori_loop(0, blocks, one, carry)

    lax.fori_loop(1, nz, drain_far, 0)


def trace_kernel(rows, t_group, gain, helped, level, taken, table, u, given, out, sparse):
    ready = (pl.program_id(0) < helped) & (taken[0] > 0)

    @pl.when(ready)
    def _():
        out[...] = given[...]

    @pl.when(jnp.logical_not(ready))
    def _():
        make_traces(u, table, level[0], gain, rows, t_group, sparse, out)


def body(nx, nz, data, estimate, window_data, wavelet, positions, bins, threshold, step):
    _, nf, lines, width = data.shape
    rows = estimate.shape[2]
    shots = window_data.shape[3]
    nchunk = nf // FC
    norm = 1.0 / math.sqrt(shots * RCV)
    fi, cols = FC * rows, nx * FC * lines
    mz = lax.axis_index("freq")
    nt = NT // nz
    blocks, groups = width // BLOCK, nz * nchunk
    helped = blocks // 2 if nz >= 4 else 0
    held = max(helped, 1)
    gain, t_group = math.sqrt(RCV / NF), 32
    level = threshold.astype(jnp.float32) / 64.0

    def table_of(z):
        times = z * nt + lax.iota(jnp.int32, nt)
        phase = times[:, None] * bins[None, :] % NT
        angle = 2.0 * math.pi / NT * phase.astype(jnp.float32)
        table = jnp.stack([jnp.cos(angle), -jnp.sin(angle)], axis=1).astype(jnp.bfloat16)
        table = table.reshape(nt, 2, groups, FC).transpose(0, 2, 1, 3)
        return table.reshape(nt, 2 * nz * nf)

    vmem = pl.BlockSpec(memory_space=pltpu.VMEM)
    smem = pl.BlockSpec(memory_space=pltpu.SMEM)
    hbm = pl.BlockSpec(memory_space=pl.ANY)
    dma = pltpu.SemaphoreType.DMA
    spectra, given = pl.pallas_call(
        partial(
            update_kernel, nx, nz, nchunk, rows, lines, norm, blocks, helped, gain, t_group
        ),
        out_shape=(
            jax.ShapeDtypeStruct((blocks, nz, nchunk, 2 * fi, BLOCK), jnp.bfloat16),
            jax.ShapeDtypeStruct((held, nt * rows, BLOCK), jnp.bfloat16),
        ),
        in_specs=[vmem, vmem, vmem, smem, vmem, smem, smem, vmem],
        out_specs=(hbm, hbm),
        scratch_shapes=[
            pltpu.VMEM((nchunk, 2, cols, width), jnp.bfloat16),
            pltpu.VMEM((nchunk, 2 * fi, width), jnp.bfloat16),
            pltpu.VMEM((nchunk, blocks, 2 * fi, BLOCK), jnp.bfloat16),
            pltpu.VMEM((nchunk, 2, rows, FC, cols), jnp.float32),
            pltpu.VMEM((nchunk, 2, rows, FC, cols), jnp.float32),
            pltpu.VMEM((nz, nchunk, 2 * fi, BLOCK), jnp.bfloat16),
            pltpu.VMEM((rows, nt, BLOCK), jnp.bfloat16),
            pltpu.VMEM((held, nt * rows, BLOCK), jnp.bfloat16),
            dma((nx, nchunk)), dma((nx, nchunk)),
            dma((nchunk,)), dma((nchunk,)),
            dma((2, nz, nchunk)), dma((2, nz, nchunk)),
            dma((2, nz, nchunk)), dma((2, nz, nchunk)),
            dma((2, nz, blocks)), dma((2, nz, blocks)),
            dma((held,)), dma((held,)),
            dma((nchunk,)), dma,
        ],
        compiler_params=pltpu.CompilerParams(
            collective_id=0, has_side_effects=True, vmem_limit_bytes=58 << 20
        ),
        name="update",
    )(
        data.reshape(2, nf * lines, width),
        estimate.reshape(2, nf * rows, width),
        window_data.reshape(2, nf * rows, shots),
        wavelet,
        positions[:, None],
        step,
        level,
        table_of(jnp.where(mz < nz // 2, 0, nz - 1)),
    )
    taken = ((mz == 0) | (mz == nz - 1)).astype(jnp.int32)[None]
    traces = pl.pallas_call(
        partial(trace_kernel, rows, t_group, gain, helped),
        out_shape=jax.ShapeDtypeStruct((nt * rows, width), jnp.bfloat16),
        grid=(blocks,),
        in_specs=[
            smem,
            smem,
            pl.BlockSpec((nt, 2 * nz * nf), lambda j: (0, 0)),
            pl.BlockSpec((None, groups, 2 * fi, BLOCK), lambda j: (j, 0, 0, 0)),
            pl.BlockSpec(
                (None, nt * rows, BLOCK), lambda j: (jnp.minimum(j, held - 1), 0, 0)
            ),
        ],
        out_specs=pl.BlockSpec((nt * rows, BLOCK), lambda j: (0, j)),
        scratch_shapes=[pltpu.VMEM((rows, nt, BLOCK), jnp.bfloat16)],
        compiler_params=pltpu.CompilerParams(vmem_limit_bytes=60 << 20),
        name="traces",
    )(level, taken, table_of(mz), spectra.reshape(blocks, groups, 2 * fi, BLOCK), given)
    return traces.reshape(nt, rows, width)


def solution(mesh):
    return jax.shard_map(
        partial(body, mesh.shape["shot"], mesh.shape["freq"]),
        mesh=mesh,
        in_specs=(
            P(None, "freq", ("grp", "shot"), "rcv"),
            P(None, "freq", ("grp", "shot"), "rcv"),
            P(None, "freq", ("grp", "shot"), None),
            P(None, ("grp", "freq")),
            P(("grp", "shot")),
            P("grp"),
            P("grp"),
            P("grp"),
        ),
        out_specs=P("freq", ("grp", "shot"), "rcv"),
        check_vma=False,
    )
```

```python
from functools import partial
import math

import jax
import jax.numpy as jnp
from jax import lax
from jax.experimental import pallas as pl
from jax.experimental.pallas import tpu as pltpu
from jax.sharding import PartitionSpec as P

NF = 256
RCV = 4096
NT = 1024
FC = 8
BLOCK = 256
LAG = 1
MESH = pl.DeviceIdType.MESH


def iota(shape, dim):
    return lax.broadcasted_iota(jnp.int32, shape, dim)


def make_traces(u, table, lv, gain, rows, t_group, sparse, out):
    groups, _, width = u.shape
    part = 2 * FC
    nt = table.shape[0]
    for i in range(rows):
        ui = u[:, i * part:(i + 1) * part, :].reshape(groups * part, width)
        tr = jnp.dot(table[...], ui, preferred_element_type=jnp.float32) * gain
        sparse[i] = (jnp.maximum(tr - lv, 0.0) + jnp.minimum(tr + lv, 0.0)).astype(jnp.bfloat16)
    n = t_group * rows
    dst, src = iota((n, n), 0), iota((n, n), 1)
    perm = (src == (dst % rows) * t_group + dst // rows).astype(jnp.bfloat16)
    for g in range(nt // t_group):
        x = sparse[:, g * t_group:(g + 1) * t_group, :].reshape(n, width)
        out[g * n:(g + 1) * n, :] = jnp.dot(
            perm, x, preferred_element_type=jnp.float32
        ).astype(jnp.bfloat16)


def update_kernel(
    nx, nz, nchunk, rows, lines, norm, blocks, helped, gain, t_group,
    data, est, win, wav, pos, step, level, table, out, given,
    down, est_p, upd, mod_mine, mod_other, ubuf, sparse, made,
    x_send, x_recv, c_send, c_recv, za_send, za_recv, zb_send, zb_recv,
    zc_send, zc_recv, g_send, g_recv, own_sem, ubuf_sem,
):
    mx = lax.axis_index("shot")
    mz = lax.axis_index("freq")
    mc = lax.axis_index("rcv")
    width = data.shape[2]
    fl = FC * lines
    fi = FC * rows

    barrier = pltpu.get_barrier_semaphore()
    for d in range(1, nx):
        pl.semaphore_signal(
            barrier, inc=1, device_id={"shot": lax.rem(mx + d, nx)}, device_id_type=MESH
        )
    pl.semaphore_signal(barrier, inc=1, device_id={"rcv": 1 - mc}, device_id_type=MESH)

    @pl.when(mz > 0)
    def _():
        pl.semaphore_signal(barrier, inc=1, device_id={"freq": mz - 1}, device_id_type=MESH)

    @pl.when(mz < nz - 1)
    def _():
        pl.semaphore_signal(barrier, inc=1, device_id={"freq": mz + 1}, device_id_type=MESH)

    ends = (mz > 0).astype(jnp.int32) + (mz < nz - 1).astype(jnp.int32)
    pl.semaphore_wait(barrier, nx + ends)

    def x_copy(d, k):
        piece = down.at[k, :, pl.ds(mx * fl, fl)]
        return pltpu.make_async_remote_copy(
            src_ref=piece, dst_ref=piece,
            send_sem=x_send.at[d, k], recv_sem=x_recv.at[d, k],
            device_id={"shot": lax.rem(mx + d, nx)}, device_id_type=MESH,
        )

    def c_copy(k):
        return pltpu.make_async_remote_copy(
            src_ref=mod_mine.at[k], dst_ref=mod_other.at[k],
            send_sem=c_send.at[k], recv_sem=c_recv.at[k],
            device_id={"rcv": 1 - mc}, device_id_type=MESH,
        )

    def w_of(way):
        return 0 if way > 0 else 1

    def last(z, way):
        return z == (nz - 1 if way > 0 else 0)

    def a_copy(src, slot, k, way):
        return pltpu.make_async_remote_copy(
            src_ref=src, dst_ref=out.at[pl.ds(0, helped), slot, k],
            send_sem=za_send.at[w_of(way), slot, k], recv_sem=za_recv.at[w_of(way), slot, k],
            device_id={"freq": mz + way}, device_id_type=MESH,
        )

    def b_copy(src, slot, k, way):
        return pltpu.make_async_remote_copy(
            src_ref=src, dst_ref=out.at[pl.ds(helped, blocks - helped), slot, k],
            send_sem=zb_send.at[w_of(way), slot, k], recv_sem=zb_recv.at[w_of(way), slot, k],
            device_id={"freq": mz + way}, device_id_type=MESH,
        )

    def block_copy(slot, b, way):
        piece = out.at[b, slot]
        return pltpu.make_async_remote_copy(
            src_ref=piece, dst_ref=piece,
            send_sem=zc_send.at[w_of(way), slot, b], recv_sem=zc_recv.at[w_of(way), slot, b],
            device_id={"freq": mz + way}, device_id_type=MESH,
        )

    def given_copy(b, way):
        return pltpu.make_async_remote_copy(
            src_ref=made.at[b], dst_ref=given.at[b],
            send_sem=g_send.at[b], recv_sem=g_recv.at[b],
            device_id={"freq": mz + way}, device_id_type=MESH,
        )

    a_own = lambda k: upd.at[k, pl.ds(0, helped)]
    b_own = lambda k: upd.at[k, pl.ds(helped, blocks - helped)]
    a_out = lambda slot, k: out.at[pl.ds(0, helped), slot, k]
    b_out = lambda slot, k: out.at[pl.ds(helped, blocks - helped), slot, k]

    def own_copy(k):
        return pltpu.make_async_copy(upd.at[k], out.at[:, mz, k], own_sem.at[k])

    column = mc * width + iota((lines, width), 1)
    select = (column == pos[:, :]).astype(jnp.float32)

    def make_down(k, carry):
        for c in range(2):
            parts = []
            lines_k = data[c, pl.ds(pl.multiple_of(k * fl, fl), fl)].astype(jnp.float32)
            for f in range(FC):
                w = wav[c, k * FC + f]
                parts.append(w * select - lines_k[f * lines:(f + 1) * lines])
            down[k, c, pl.ds(pl.multiple_of(mx * fl, fl), fl)] = jnp.concatenate(
                parts, axis=0
            ).astype(jnp.bfloat16)
        for d in range(1, nx):
            x_copy(d, k).start()
        return carry

    lax.fori_loop(0, nchunk, make_down, 0)

    n = 2 * fi
    dst, src = iota((n, n), 0), iota((n, n), 1)
    want = (dst // FC % 2) * fi + (dst % FC) * rows + dst // (2 * FC)
    perm = (src == want).astype(jnp.bfloat16)

    def chunk_of(ref, k):
        part = pl.ds(pl.multiple_of(k * fi, fi), fi)
        return jnp.concatenate([ref[0, part], ref[1, part]], axis=0)

    def permute(k, carry):
        est_p[k] = jnp.dot(
            perm, chunk_of(est, k), preferred_element_type=jnp.float32
        ).astype(jnp.bfloat16)
        return carry

    lax.fori_loop(0, nchunk, permute, 0)

    cols = nx * fl
    shots = win.shape[2]
    s_row, s_col = iota((shots, cols), 0), iota((shots, cols), 1)
    spread = (s_row == (s_col // fl) * lines + s_col % lines).astype(jnp.bfloat16)
    shape3 = (rows, FC, cols)
    same = iota(shape3, 1) == iota(shape3, 2) % fl // lines
    scale = step[0]

    def model(k):
        for d in range(1, nx):
            here = down.at[k, :, pl.ds(lax.rem(mx + nx - d, nx) * fl, fl)]
            pltpu.make_async_remote_copy(
                src_ref=here, dst_ref=here,
                send_sem=x_send.at[d, k], recv_sem=x_recv.at[d, k],
                device_id={"shot": lax.rem(mx + d, nx)}, device_id_type=MESH,
            ).wait_recv()
        lines_k = down[k].reshape(2 * cols, width)
        m = lax.dot_general(
            est_p[k], lines_k, (((1,), (1,)), ((), ())), preferred_element_type=jnp.float32
        ).reshape(rows, 2, FC, 2 * cols)
        mod_mine[k, 0] = m[:, 0, :, :cols] - m[:, 1, :, cols:]
        mod_mine[k, 1] = m[:, 0, :, cols:] + m[:, 1, :, :cols]
        c_copy(k).start()

    def update(k):
        c_copy(k).wait_recv()
        total_re = mod_mine[k, 0] + mod_other[k, 0]
        total_im = mod_mine[k, 1] + mod_other[k, 1]
        w = jnp.dot(perm, chunk_of(win, k), preferred_element_type=jnp.float32).astype(jnp.bfloat16)
        w = jnp.dot(w, spread, preferred_element_type=jnp.float32).reshape(rows, 2, FC, cols)
        e_re = jnp.where(same, w[:, 0] - total_re, 0.0)
        e_im = jnp.where(same, w[:, 1] - total_im, 0.0)
        e = jnp.stack(
            [jnp.concatenate([e_re, e_im], axis=2), jnp.concatenate([e_im, -e_re], axis=2)], axis=1
        ).reshape(n, 2 * cols).astype(jnp.bfloat16)
        grad = jnp.dot(e, down[k].reshape(2 * cols, width), preferred_element_type=jnp.float32)
        new = (est_p[k].astype(jnp.float32) - scale * (grad * norm)).astype(jnp.bfloat16)
        for b in range(blocks):
            upd[k, b] = new[:, b * BLOCK:(b + 1) * BLOCK]
        own_copy(k).start()
        for way in (1, -1):
            @pl.when(jnp.logical_not(last(mz, way)))
            def _():
                b_copy(b_own(k), mz, k, way).start()

                if helped:
                    @pl.when(jnp.logical_not(last(mz + way, way)))
                    def _():
                        a_copy(a_own(k), mz, k, way).start()

    def near(k):
        for way in (1, -1):
            slot = mz - way

            @pl.when((slot >= 0) & (slot < nz))
            def _():
                b_copy(b_out(slot, k), slot, k, way).wait_recv()

                if helped:
                    @pl.when(jnp.logical_not(last(mz, way)))
                    def _():
                        a_copy(a_out(slot, k), slot, k, way).wait_recv()

                @pl.when(last(mz + way, way))
                def _():
                    b_copy(b_out(slot, k), slot, k, way).start()

    def step_of(k, carry):
        @pl.when(k < nchunk)
        def _():
            model(k)
            update(k)

        @pl.when(k >= LAG)
        def _():
            near(k - LAG)

        return carry

    lax.fori_loop(0, nchunk + LAG, step_of, 0)

    def own_done(k, carry):
        own_copy(k).wait()
        return carry

    lax.fori_loop(0, nchunk, own_done, 0)

    def hand_on(b, carry):
        for way in (1, -1):
            slot = mz - way
            inside = (slot >= 0) & (slot < nz)
            nxt = mz + way

            @pl.when(inside & (nxt > 0) & (nxt < nz - 1))
            def _():
                block_copy(slot, b, way).start()

        return carry

    lax.fori_loop(0, blocks, hand_on, 0)

    def far(h, carry):
        def one(b, carry):
            for way in (1, -1):
                slot = mz - way * h
                nxt = mz + way
                inside = (slot >= 0) & (slot < nz)
                at_end = last(mz, way)

                @pl.when(inside & jnp.logical_not(at_end))
                def _():
                    block_copy(slot, b, way).wait_recv()

                    @pl.when(jnp.logical_not(last(nxt, way)) | (b >= helped))
                    def _():
                        block_copy(slot, b, way).start()

                    if helped:
                        @pl.when(last(nxt, way) & (b < helped) & last(slot, -way))
                        def _():
                            load = pltpu.make_async_copy(out.at[b], ubuf, ubuf_sem)
                            load.start()
                            load.wait()
                            make_traces(
                                ubuf.reshape(nz * nchunk, ubuf.shape[2], BLOCK), table, level[0],
                                gain, rows, t_group, sparse, made.at[b],
                            )
                            given_copy(b, way).start()

                @pl.when(inside & at_end & (b >= helped))
                def _():
                    if not near_by:
                        block_copy(slot, b, way).wait_recv()

            return carry

        near_by = isinstance(h, int)
        return lax.fori_loop(0, blocks, one, carry)

    def end_chunk(k, carry):
        for way in (1, -1):
            slot = mz - 2 * way

            @pl.when((slot >= 0) & (slot < nz) & last(mz, way))
            def _():
                b_copy(b_out(slot, k), slot, k, way).wait_recv()

        return carry

    if nz > 2:
        lax.fori_loop(0, nchunk, end_chunk, 0)
        far(2, 0)
    lax.fori_loop(3, nz, far, 0)

    if helped:
        def take(b, carry):
            for way in (1, -1):
                @pl.when(last(mz, way))
                def _():
                    given_copy(b, way).wait_recv()

                @pl.when(last(mz + way, way))
                def _():
                    given_copy(b, way).wait_send()

            return carry

        lax.fori_loop(0, helped, take, 0)

    def drain(k, carry):
        for d in range(1, nx):
            x_copy(d, k).wait_send()
        c_copy(k).wait_send()
        for way in (1, -1):
            nxt = mz + way

            @pl.when(jnp.logical_not(last(mz, way)))
            def _():
                b_copy(b_own(k), mz, k, way).wait_send()

                if helped:
                    @pl.when(jnp.logical_not(last(nxt, way)))
                    def _():
                        a_copy(a_own(k), mz, k, way).wait_send()

            slot = mz - way

            @pl.when((slot >= 0) & (slot < nz) & last(nxt, way))
            def _():
                b_copy(b_own(k), slot, k, way).wait_send()

        return carry

    lax.fori_loop(0, nchunk, drain, 0)

    def drain_far(h, carry):
        def one(b, carry):
            for way in (1, -1):
                slot = mz - way * h
                nxt = mz + way
                inside = (slot >= 0) & (slot < nz) & (nxt >= 0) & (nxt < nz)
                to_end = last(nxt, way)

                @pl.when(inside & (jnp.logical_not(to_end) | ((b >= helped) & (h > 1))))
                def _():
                    block_copy(slot, b, way).wait_send()

            return carry

        return lax.fori_loop(0, blocks, one, carry)

    lax.fori_loop(1, nz, drain_far, 0)


def trace_kernel(rows, t_group, gain, helped, level, taken, table, u, given, out, sparse):
    ready = (pl.program_id(0) < helped) & (taken[0] > 0)

    @pl.when(ready)
    def _():
        out[...] = given[...]

    @pl.when(jnp.logical_not(ready))
    def _():
        make_traces(u, table, level[0], gain, rows, t_group, sparse, out)


def body(nx, nz, data, estimate, window_data, wavelet, positions, bins, threshold, step):
    _, nf, lines, width = data.shape
    rows = estimate.shape[2]
    shots = window_data.shape[3]
    nchunk = nf // FC
    norm = 1.0 / math.sqrt(shots * RCV)
    fi, cols = FC * rows, nx * FC * lines
    mz = lax.axis_index("freq")
    nt = NT // nz
    blocks, groups = width // BLOCK, nz * nchunk
    helped = 3 * blocks // 8 if nz >= 4 else 0
    held = max(helped, 1)
    gain, t_group = math.sqrt(RCV / NF), 32
    level = threshold.astype(jnp.float32) / 64.0

    def table_of(z):
        times = z * nt + lax.iota(jnp.int32, nt)
        phase = times[:, None] * bins[None, :] % NT
        angle = 2.0 * math.pi / NT * phase.astype(jnp.float32)
        table = jnp.stack([jnp.cos(angle), -jnp.sin(angle)], axis=1).astype(jnp.bfloat16)
        table = table.reshape(nt, 2, groups, FC).transpose(0, 2, 1, 3)
        return table.reshape(nt, 2 * nz * nf)

    vmem = pl.BlockSpec(memory_space=pltpu.VMEM)
    smem = pl.BlockSpec(memory_space=pltpu.SMEM)
    hbm = pl.BlockSpec(memory_space=pl.ANY)
    dma = pltpu.SemaphoreType.DMA
    spectra, given = pl.pallas_call(
        partial(
            update_kernel, nx, nz, nchunk, rows, lines, norm, blocks, helped, gain, t_group
        ),
        out_shape=(
            jax.ShapeDtypeStruct((blocks, nz, nchunk, 2 * fi, BLOCK), jnp.bfloat16),
            jax.ShapeDtypeStruct((held, nt * rows, BLOCK), jnp.bfloat16),
        ),
        in_specs=[vmem, vmem, vmem, smem, vmem, smem, smem, vmem],
        out_specs=(hbm, hbm),
        scratch_shapes=[
            pltpu.VMEM((nchunk, 2, cols, width), jnp.bfloat16),
            pltpu.VMEM((nchunk, 2 * fi, width), jnp.bfloat16),
            pltpu.VMEM((nchunk, blocks, 2 * fi, BLOCK), jnp.bfloat16),
            pltpu.VMEM((nchunk, 2, rows, FC, cols), jnp.float32),
            pltpu.VMEM((nchunk, 2, rows, FC, cols), jnp.float32),
            pltpu.VMEM((nz, nchunk, 2 * fi, BLOCK), jnp.bfloat16),
            pltpu.VMEM((rows, nt, BLOCK), jnp.bfloat16),
            pltpu.VMEM((held, nt * rows, BLOCK), jnp.bfloat16),
            dma((nx, nchunk)), dma((nx, nchunk)),
            dma((nchunk,)), dma((nchunk,)),
            dma((2, nz, nchunk)), dma((2, nz, nchunk)),
            dma((2, nz, nchunk)), dma((2, nz, nchunk)),
            dma((2, nz, blocks)), dma((2, nz, blocks)),
            dma((held,)), dma((held,)),
            dma((nchunk,)), dma,
        ],
        compiler_params=pltpu.CompilerParams(
            collective_id=0, has_side_effects=True, vmem_limit_bytes=58 << 20
        ),
        name="update",
    )(
        data.reshape(2, nf * lines, width),
        estimate.reshape(2, nf * rows, width),
        window_data.reshape(2, nf * rows, shots),
        wavelet,
        positions[:, None],
        step,
        level,
        table_of(jnp.where(mz < nz // 2, 0, nz - 1)),
    )
    taken = ((mz == 0) | (mz == nz - 1)).astype(jnp.int32)[None]
    traces = pl.pallas_call(
        partial(trace_kernel, rows, t_group, gain, helped),
        out_shape=jax.ShapeDtypeStruct((nt * rows, width), jnp.bfloat16),
        grid=(blocks,),
        in_specs=[
            smem,
            smem,
            pl.BlockSpec((nt, 2 * nz * nf), lambda j: (0, 0)),
            pl.BlockSpec((None, groups, 2 * fi, BLOCK), lambda j: (j, 0, 0, 0)),
            pl.BlockSpec(
                (None, nt * rows, BLOCK), lambda j: (jnp.minimum(j, held - 1), 0, 0)
            ),
        ],
        out_specs=pl.BlockSpec((nt * rows, BLOCK), lambda j: (0, j)),
        scratch_shapes=[pltpu.VMEM((rows, nt, BLOCK), jnp.bfloat16)],
        compiler_params=pltpu.CompilerParams(vmem_limit_bytes=60 << 20),
        name="traces",
    )(level, taken, table_of(mz), spectra.reshape(blocks, groups, 2 * fi, BLOCK), given)
    return traces.reshape(nt, rows, width)


def solution(mesh):
    return jax.shard_map(
        partial(body, mesh.shape["shot"], mesh.shape["freq"]),
        mesh=mesh,
        in_specs=(
            P(None, "freq", ("grp", "shot"), "rcv"),
            P(None, "freq", ("grp", "shot"), "rcv"),
            P(None, "freq", ("grp", "shot"), None),
            P(None, ("grp", "freq")),
            P(("grp", "shot")),
            P("grp"),
            P("grp"),
            P("grp"),
        ),
        out_specs=P("freq", ("grp", "shot"), "rcv"),
        check_vma=False,
    )
```
